32 devices in a mesh: col: 8 (over z, y), row: 4 (over x, core).
Axes of the slice: x: 2, y: 2, z: 4, core: 2. Of those that a mesh axis runs over, the one named last changes fastest.
Arguments:
- hamiltonian: float32 [16384, 16384], P('row', 'col'), as said below
Outputs:
- reduced: float32 [16384, 16384], P('row', 'col')
Inputs may be any that keep to these rules, and one draw needn't show every extreme that they name: hamiltonian is symmetric.
All inputs are finite; a program needn't handle non-finite values.
Results may differ from the reference program's by a relative error of at most 0.00019.
Values sent between devices are 32-bit elements; how exact they have to be, the bound alone decides.
A program may use at most 192 MiB of HBM per device.

```python
import jax
import jax.numpy as jnp
from jax import lax

M = 16384
NB = 256
PANELS = 2


def draw_hamiltonian(key, part):
    first_key = jax.random.fold_in(jax.random.fold_in(key, 11), 0)
    noise = jax.random.normal(first_key, (M, M), jnp.float32)
    sym = (noise + noise.T) * 0.7071
    return sym


def setup_inputs(seed: int = 0) -> dict:
    streams_of = jax.random.split(jax.random.key(seed), 2)
    return {
        "hamiltonian": draw_hamiltonian(jax.random.fold_in(streams_of[1], 71), 0),
    }


def product(left, right):
    return jnp.dot(left.astype(jnp.float32), right.astype(jnp.float32), precision=lax.Precision.HIGHEST, preferred_element_type=jnp.float32)

def inner_tn(left, right):
    return lax.dot_general(left.astype(jnp.float32), right.astype(jnp.float32), (((0,), (0,)), ((), ())), precision=lax.Precision.HIGHEST, preferred_element_type=jnp.float32)

def outer_nt(left, right):
    return lax.dot_general(left.astype(jnp.float32), right.astype(jnp.float32), (((1,), (1,)), ((), ())), precision=lax.Precision.HIGHEST, preferred_element_type=jnp.float32)

def normalize(panel):
    gram = inner_tn(panel, panel)
    lower = jnp.linalg.cholesky(gram)
    return lax.linalg.triangular_solve(lower, panel, left_side=False, lower=True, transpose_a=True)

def coupling_of(top_rows):
    square = jnp.eye(NB, dtype=top_rows.dtype) - top_rows.T
    normal_eq = inner_tn(square, square)
    factor = jnp.linalg.cholesky(normal_eq)
    middle = lax.linalg.triangular_solve(factor, square.T, left_side=True, lower=True)
    return lax.linalg.triangular_solve(factor, middle, left_side=True, lower=True, transpose_a=True)

def reduce_panel(matrix, first_col):
    first_row = first_col + NB
    row_ids = jnp.arange(M, dtype=jnp.int32)
    live = (row_ids >= first_row)[:, None]
    panel = jnp.where(live, matrix[:, first_col:first_col + NB], jnp.zeros((), matrix.dtype))
    basis = normalize(panel)
    coupling = coupling_of(basis[first_row:first_row + NB])
    ident = (row_ids[:, None] - first_row == jnp.arange(NB, dtype=jnp.int32)[None, :]).astype(matrix.dtype)
    vectors = ident - basis
    applied = product(product(matrix, vectors), coupling)
    inner = product(coupling.T, inner_tn(vectors, applied))
    shifted = applied - 0.5 * product(vectors, inner)
    return matrix - outer_nt(vectors, shifted) - outer_nt(shifted, vectors)

def reference(hamiltonian):
    matrix = hamiltonian
    for panel_index in range(PANELS):
        matrix = reduce_panel(matrix, panel_index * NB)
    return matrix
```

```python
import jax
import jax.numpy as jnp
from jax import lax
from jax.sharding import PartitionSpec as P

NB = 256
PANELS = 2
CHUNKS = 2
BOTH = ("col", "row")


def mm(left, right, dims, precision=lax.Precision.HIGHEST):
    return lax.dot_general(
        left,
        right,
        ((dims[0], dims[1]), ((), ())),
        precision=precision,
        preferred_element_type=jnp.float32,
    )


def nn(left, right, precision=lax.Precision.HIGHEST):
    return mm(left, right, ((1,), (0,)), precision)


def nt(left, right, precision=lax.Precision.HIGHEST):
    return mm(left, right, ((1,), (1,)), precision)


def tn(left, right, precision=lax.Precision.HIGHEST):
    return mm(left, right, ((0,), (0,)), precision)


def inverse_factor(gram):
    lower = jnp.linalg.cholesky(gram)
    eye = jnp.eye(NB, dtype=jnp.float32)
    return lax.linalg.triangular_solve(lower, eye, left_side=True, lower=True)


def small_factors(gram, top):
    inv = inverse_factor(gram)
    basis_top = nt(top, inv)
    square = jnp.eye(NB, dtype=jnp.float32) - basis_top.T
    inv2 = inverse_factor(tn(square, square))
    coupling = tn(inv2, nt(inv2, square))
    return inv, basis_top, coupling


def to_rows(block, rows, ratio):
    swap = [
        ((ratio * i + q) * rows + s, (ratio * s + q) * rows + i)
        for s in range(rows)
        for i in range(rows)
        for q in range(ratio)
    ]
    place = lax.axis_index("col") % ratio
    height = block.shape[0] // CHUNKS
    out = []
    for chunk in range(CHUNKS):
        own = lax.ppermute(block[chunk * height : (chunk + 1) * height], BOTH, swap)
        parts = [own]
        for step in range(1, ratio):
            turn = [
                (ratio * s + q, ratio * s + (q + step) % ratio)
                for s in range(rows)
                for q in range(ratio)
            ]
            parts.append(lax.ppermute(own, "col", turn))
        ordered = []
        for q in range(ratio):
            piece = parts[0]
            for step in range(1, ratio):
                piece = jnp.where((place - q) % ratio == step, parts[step], piece)
            ordered.append(piece)
        out.append(jnp.concatenate(ordered, axis=1))
    return jnp.concatenate(out, axis=0)


def unit_rows(ids, first_row):
    return (jnp.arange(NB, dtype=jnp.int32)[:, None] + first_row == ids[None, :]).astype(jnp.float32)


def shards(matrix):
    row_block, col_block = matrix.shape
    rows = lax.axis_size("row")
    ratio = lax.axis_size("col") // rows
    row_pos = lax.axis_index("row")
    col_pos = lax.axis_index("col")
    row_ids = row_pos * row_block + jnp.arange(row_block, dtype=jnp.int32)
    col_ids = col_pos * col_block + jnp.arange(col_block, dtype=jnp.int32)
    high = lax.Precision.HIGH

    def from_first_row(block):
        return lax.psum(jnp.where(row_pos == 0, block, 0.0), "row")

    def columns_of(block, first):
        start = first % col_block
        return jnp.where(col_pos == first // col_block, block[:, start : start + NB], 0.0)

    first_c = from_first_row(matrix[:NB])
    panel = jnp.where((row_ids >= NB)[:, None], matrix[:, :NB], 0.0)
    top = jnp.where(row_pos == 0, matrix[NB : 2 * NB, :NB], 0.0)
    sums = lax.psum(jnp.where(col_pos == 0, jnp.concatenate([tn(panel, panel), top]), 0.0), BOTH)
    first_r = to_rows(first_c, rows, ratio)
    second_c = from_first_row(lax.optimization_barrier((matrix[NB : 2 * NB], first_c))[0])
    second_r = to_rows(lax.optimization_barrier((second_c, first_r))[0], rows, ratio)

    inv, basis_top, coupling = small_factors(sums[:NB], sums[NB:])
    v1_r = unit_rows(row_ids, NB) - nn(inv, jnp.where(row_ids >= NB, first_r, 0.0))
    v1_c = unit_rows(col_ids, NB) - nn(inv, jnp.where(col_ids >= NB, first_c, 0.0))
    partial = nn(v1_r, matrix, high)
    z_c = lax.psum(partial, "row")
    z_top = columns_of(partial, NB)
    sums = lax.psum(jnp.concatenate([nt(v1_c, partial), z_top]), BOTH)
    v1_top = jnp.eye(NB, dtype=jnp.float32) - basis_top
    inner = nn(tn(coupling, sums[:NB]), coupling)
    s1_top = tn(sums[NB:], coupling) - 0.5 * nn(v1_top, inner)
    s1_c = tn(coupling, z_c) - 0.5 * tn(inner, v1_c)

    p2_c = second_c - nn(s1_top, v1_c) - nn(v1_top, s1_c)
    p2_c = jnp.where(col_ids >= 2 * NB, p2_c, 0.0)
    top = columns_of(p2_c, 2 * NB).T
    sums = lax.psum(jnp.concatenate([nt(p2_c, p2_c), top]), "col")
    s1_r = to_rows(s1_c, rows, ratio)
    p2_r = second_r - nn(s1_top, v1_r) - nn(v1_top, s1_r)
    p2_r = jnp.where(row_ids >= 2 * NB, p2_r, 0.0)

    inv, basis_top, coupling = small_factors(sums[:NB], sums[NB:])
    v2_r = unit_rows(row_ids, 2 * NB) - nn(inv, p2_r)
    v2_c = unit_rows(col_ids, 2 * NB) - nn(inv, p2_c)
    partial = nn(v2_r, matrix, high) - nn(nt(v2_r, s1_r), v1_c) - nn(nt(v2_r, v1_r), s1_c)
    z_c = lax.psum(partial, "row")
    inner = lax.psum(nt(v2_c, partial), BOTH)
    inner = nn(tn(coupling, inner), coupling)
    s2_c = tn(coupling, z_c) - 0.5 * tn(inner, v2_c)
    s2_r = to_rows(s2_c, rows, ratio)

    early = tn(
        jnp.concatenate([v1_r, s1_r, v2_r]), jnp.concatenate([s1_c, v1_c, s2_c]), high
    )
    return (matrix - early) - tn(s2_r, v2_c, high)


def solution(mesh):
    return jax.shard_map(
        shards,
        mesh=mesh,
        in_specs=(P("row", "col"),),
        out_specs=P("row", "col"),
        check_vma=False,
    )
```

```python
import jax
import jax.numpy as jnp
from jax import lax
from jax.sharding import PartitionSpec as P

NB = 256
PANELS = 2
CHUNKS = 2
BOTH = ("col", "row")


def mm(left, right, dims, precision=lax.Precision.HIGHEST):
    return lax.dot_general(
        left,
        right,
        ((dims[0], dims[1]), ((), ())),
        precision=precision,
        preferred_element_type=jnp.float32,
    )


def nn(left, right, precision=lax.Precision.HIGHEST):
    return mm(left, right, ((1,), (0,)), precision)


def nt(left, right, precision=lax.Precision.HIGHEST):
    return mm(left, right, ((1,), (1,)), precision)


def tn(left, right, precision=lax.Precision.HIGHEST):
    return mm(left, right, ((0,), (0,)), precision)


def inverse_factor(gram):
    lower = jnp.linalg.cholesky(gram)
    eye = jnp.eye(NB, dtype=jnp.float32)
    return lax.linalg.triangular_solve(lower, eye, left_side=True, lower=True)


def small_factors(gram, top):
    inv = inverse_factor(gram)
    basis_top = nt(top, inv)
    square = jnp.eye(NB, dtype=jnp.float32) - basis_top.T
    inv2 = inverse_factor(tn(square, square))
    coupling = tn(inv2, nt(inv2, square))
    return inv, basis_top, coupling


def to_rows(block, rows, ratio):
    swap = [
        ((ratio * i + q) * rows + s, (ratio * s + q) * rows + i)
        for s in range(rows)
        for i in range(rows)
        for q in range(ratio)
    ]
    place = lax.axis_index("col") % ratio
    height = block.shape[0] // CHUNKS
    out = []
    for chunk in range(CHUNKS):
        own = lax.ppermute(block[chunk * height : (chunk + 1) * height], BOTH, swap)
        parts = [own]
        for step in range(1, ratio):
            turn = [
                (ratio * s + q, ratio * s + (q + step) % ratio)
                for s in range(rows)
                for q in range(ratio)
            ]
            parts.append(lax.ppermute(own, "col", turn))
        ordered = []
        for q in range(ratio):
            piece = parts[0]
            for step in range(1, ratio):
                piece = jnp.where((place - q) % ratio == step, parts[step], piece)
            ordered.append(piece)
        out.append(jnp.concatenate(ordered, axis=1))
    return jnp.concatenate(out, axis=0)


def exchange(block, axis, bit):
    size = lax.axis_size(axis)
    return lax.ppermute(block, axis, [(k, k ^ bit) for k in range(size)])


def scatter_over_rows(block):
    bit = 1
    while bit < lax.axis_size("row"):
        upper = (lax.axis_index("row") & bit) != 0
        half = block.shape[0] // 2
        low, top = block[:half], block[half:]
        sent = exchange(jnp.where(upper, low, top), "row", bit)
        block = jnp.where(upper, top, low) + sent
        bit *= 2
    return block


def sum_over_cols(block):
    bit = 1
    while bit < lax.axis_size("col"):
        block = block + exchange(block, "col", bit)
        bit *= 2
    return block


def gather_over_rows(block):
    bit = lax.axis_size("row") // 2
    while bit:
        upper = (lax.axis_index("row") & bit) != 0
        other = exchange(block, "row", bit)
        block = jnp.where(
            upper, jnp.concatenate([other, block]), jnp.concatenate([block, other])
        )
        bit //= 2
    return block


def own_part(block):
    bit = 1
    while bit < lax.axis_size("row"):
        upper = (lax.axis_index("row") & bit) != 0
        half = block.shape[0] // 2
        block = jnp.where(upper, block[half:], block[:half])
        bit *= 2
    return block


def unit_rows(ids, first_row):
    return (jnp.arange(NB, dtype=jnp.int32)[:, None] + first_row == ids[None, :]).astype(jnp.float32)


def shards(matrix):
    row_block, col_block = matrix.shape
    rows = lax.axis_size("row")
    ratio = lax.axis_size("col") // rows
    row_pos = lax.axis_index("row")
    col_pos = lax.axis_index("col")
    row_ids = row_pos * row_block + jnp.arange(row_block, dtype=jnp.int32)
    col_ids = col_pos * col_block + jnp.arange(col_block, dtype=jnp.int32)
    high = lax.Precision.HIGH

    def from_first_row(block):
        return gather_over_rows(scatter_over_rows(jnp.where(row_pos == 0, block, 0.0)))

    def columns_of(block, first):
        start = first % col_block
        return jnp.where(col_pos == first // col_block, block[:, start : start + NB], 0.0)

    first_c = from_first_row(matrix[:NB])
    panel = jnp.where((row_ids >= NB)[:, None], matrix[:, :NB], 0.0)
    top = jnp.where(row_pos == 0, matrix[NB : 2 * NB, :NB], 0.0)
    sums = jnp.concatenate([tn(panel, panel), top.T], axis=1)
    sums = scatter_over_rows(jnp.where(col_pos == 0, sums, 0.0))
    sums = gather_over_rows(sum_over_cols(sums))
    first_r = to_rows(first_c, rows, ratio)
    second_c = from_first_row(lax.optimization_barrier((matrix[NB : 2 * NB], first_c))[0])
    second_r = to_rows(lax.optimization_barrier((second_c, first_r))[0], rows, ratio)

    inv, basis_top, coupling = small_factors(sums[:, :NB], sums[:, NB:].T)
    v1_r = unit_rows(row_ids, NB) - nn(inv, jnp.where(row_ids >= NB, first_r, 0.0))
    v1_c = unit_rows(col_ids, NB) - nn(inv, jnp.where(col_ids >= NB, first_c, 0.0))
    partial = nn(v1_r, matrix, high)
    z_top = columns_of(partial, NB)
    sums = scatter_over_rows(jnp.concatenate([nt(v1_c, partial), z_top, partial], axis=1))
    z_c = gather_over_rows(sums[:, 2 * NB :])
    sums = gather_over_rows(sum_over_cols(sums[:, : 2 * NB]))
    v1_top = jnp.eye(NB, dtype=jnp.float32) - basis_top
    inner = nn(tn(coupling, sums[:, :NB]), coupling)
    s1_top = tn(sums[:, NB:], coupling) - 0.5 * nn(v1_top, inner)
    s1_c = tn(coupling, z_c) - 0.5 * tn(inner, v1_c)

    p2_c = second_c - nn(s1_top, v1_c) - nn(v1_top, s1_c)
    p2_c = jnp.where(col_ids >= 2 * NB, p2_c, 0.0)
    sums = jnp.concatenate([nt(own_part(p2_c), p2_c), own_part(columns_of(p2_c, 2 * NB))], axis=1)
    sums = gather_over_rows(sum_over_cols(sums))
    s1_r = to_rows(s1_c, rows, ratio)
    p2_r = second_r - nn(s1_top, v1_r) - nn(v1_top, s1_r)
    p2_r = jnp.where(row_ids >= 2 * NB, p2_r, 0.0)

    inv, basis_top, coupling = small_factors(sums[:, :NB], sums[:, NB:].T)
    v2_r = unit_rows(row_ids, 2 * NB) - nn(inv, p2_r)
    v2_c = unit_rows(col_ids, 2 * NB) - nn(inv, p2_c)
    partial = nn(v2_r, matrix, high) - nn(nt(v2_r, s1_r), v1_c) - nn(nt(v2_r, v1_r), s1_c)
    sums = scatter_over_rows(jnp.concatenate([nt(v2_c, partial), partial], axis=1))
    z_c = gather_over_rows(sums[:, NB:])
    inner = gather_over_rows(sum_over_cols(sums[:, :NB]))
    inner = nn(tn(coupling, inner), coupling)
    s2_c = tn(coupling, z_c) - 0.5 * tn(inner, v2_c)
    s2_r = to_rows(s2_c, rows, ratio)

    early = tn(
        jnp.concatenate([v1_r, s1_r, v2_r]), jnp.concatenate([s1_c, v1_c, s2_c]), high
    )
    return (matrix - early) - tn(s2_r, v2_c, high)


def solution(mesh):
    return jax.shard_map(
        shards,
        mesh=mesh,
        in_specs=(P("row", "col"),),
        out_specs=P("row", "col"),
        check_vma=False,
    )
```
